256 devices in a mesh: expert: 64 (over z, x, y_hi), etp: 4 (over y_lo, core).
Axes of the slice: x: 4, y: 4 (y_hi: 2, y_lo: 2; y = y_hi * 2 + y_lo), z: 8, core: 2. Of those that a mesh axis runs over, the one named last changes fastest.
Arguments:
- hidden_act: bfloat16 [64, 1024, 2880], P('expert', None, 'etp'), may hold values from -6 to 6
- down_weight: bfloat16 [64, 2880, 2880], P('expert', 'etp'), may hold values from -0.109375 to 0.109375
- out_grad: bfloat16 [8192, 2880], P('expert', 'etp'), may hold values from -1.5 to 1.5
- route_probs: float32 [8192, 4], P('expert'), may hold values from 0.05 to 1
- expert_ids: int32 [8192, 4], P('expert'), may hold values from 0 to 63, all different within a row; in each aligned block of 128 rows (0 to 127, 128 to 255, ...) at most 16 rows name the same one
Outputs:
- weight_grad: bfloat16 [64, 2880, 2880], P('expert', 'etp')
- hidden_grad: bfloat16 [64, 1024, 2880], P('expert', None, 'etp')
- prob_grad: float32 [8192, 4], P('expert')
The draws below stay inside these ranges and needn't reach their ends.
Inputs may be any that keep to these rules, and one draw needn't show every extreme that they name: `expert_ids`: each token names 4 different experts; among the 128 tokens held by one device index along the mesh axis `expert` no expert is named more than 16 times, a bound that some block reaches.
All inputs are finite; a program needn't handle non-finite values.
Results may differ from the reference program's by a relative error of at most 0.015.
Values may be sent and summed in bfloat16 or wider, within the bound.
A program may use at most 128 MiB of HBM per device.

```python
import math
import jax
import jax.numpy as jnp
import numpy as np
from jax import lax

D = 2880
FF = 2880
TOP = 4
TOK_DEV = 128
EXPERTS = 64
TOKENS = 8192
CAP = 1024
C_SRC = 16


def block_levels(rng, extent, pieces, smallest, largest):
    def one(dim, shards_of):
        steps = jax.random.uniform(jax.random.fold_in(jax.random.fold_in(rng, 6), dim), (shards_of,), jnp.float32, smallest / len(pieces), largest / len(pieces))
        return jnp.repeat(jnp.exp(steps), extent[dim] // shards_of).reshape((-1,) + (1,) * (len(extent) - dim - 1))

    factor_of = one(*pieces[0])
    for cut in pieces[1:]:
        factor_of = factor_of * one(*cut)
    return factor_of


def assign_block(rng, own, number, rows, amount, top, limit, skew):
    sequence = jax.random.permutation(rng, amount)
    crowded, usual = portions_of(amount, rows * top, limit, skew, True), portions_of(amount, rows * top, limit, skew, False)
    places = jnp.arange(amount)

    def named(sizes, rotation):
        used = int((sizes > 0).sum())
        fixed = max(1, used // 4)
        moved = fixed + (places - fixed + rotation * (used - fixed)) % max(1, amount - fixed)
        return jnp.zeros((amount,), jnp.int32).at[sequence[jnp.where(places < fixed, places, moved)]].set(jnp.asarray(sizes, jnp.int32))

    sizes = jnp.where(number % 4 == 0, named(crowded, number // 4), named(usual, number - number // 4 - 1))
    mixed = jax.random.permutation(jax.random.fold_in(own, 3), amount)
    source_of, taker = mixed[0:amount // 2 * 2:2], mixed[1:amount // 2 * 2:2]
    margin = jnp.minimum(sizes[source_of] - 1, limit - sizes[taker]) // 2
    margin = jnp.where((source_of == sequence[0]) | (taker == sequence[0]) | (sizes[taker] == 0), 0, jnp.maximum(margin, 0))
    moved = jax.random.randint(jax.random.fold_in(own, 4), (amount // 2,), 0, 1 << 20) % (margin + 1)
    sizes = sizes.at[source_of].add(-moved).at[taker].add(moved)
    items = jnp.searchsorted(jnp.cumsum(sizes), jnp.arange(rows * top), side="right").astype(jnp.int32)
    grid = items.reshape(top, rows).T
    grid = grid[jax.random.permutation(jax.random.fold_in(own, 1), rows)]
    rotation = jax.random.randint(jax.random.fold_in(own, 2), (rows, 1), 0, top)
    return jnp.take_along_axis(grid, (jnp.arange(top)[None, :] + rotation) % top, axis=1)


def portions_of(amount, total, bound, lean, full):
    loads = [(1 << 20) // math.isqrt(grade ** lean) + 1 for grade in range(1, amount + 1)]
    largest = bound if full else min(bound, max(-(-total // amount), total * loads[0] // sum(loads)))
    least = 1 if total - largest >= amount - 1 else 0
    holding, surplus = [largest] + [least] * (amount - 1), total - largest - least * (amount - 1)
    while surplus > 0:
        movable = [i for i in range(1, amount) if holding[i] < largest] or [i for i in range(1, amount) if holding[i] < bound]
        whole, remaining = sum([loads[i] for i in movable]), surplus
        for i in movable:
            more = min(bound - holding[i], max(1, remaining * loads[i] // whole), surplus)
            holding[i] = holding[i] + more
            surplus = surplus - more
    return np.array(holding)


def bell_draw(own_key, dims, spread, bound, shards=(), held_as=jnp.bfloat16):
    loudness = block_levels(own_key, dims, shards, -0.22, 0.18) if shards else 1.0
    values = jax.random.normal(own_key, dims, jnp.float32) * spread * loudness
    return jnp.minimum(jnp.maximum(values, -bound), bound).astype(held_as)


def setup_inputs(seed: int = 0) -> dict:
    keys = jax.random.split(jax.random.key(seed), 6)
    hidden_act = bell_draw(keys[0], (EXPERTS, CAP, FF), 1.0, 6.0, ((0, 64), (2, 4)))
    down_weight = bell_draw(keys[1], (EXPERTS, FF, D), FF ** -0.5, 0.109375, ((0, 64), (1, 4)))
    out_grad = bell_draw(keys[2], (TOKENS, D), 0.25, 1.5, ((0, 64), (1, 4)))
    route_probs = jnp.clip(0.05 + 0.95 * jax.random.uniform(keys[3], (TOKENS, TOP), jnp.float32) ** block_levels(keys[3], (TOKENS, TOP), ((0, 64),), -0.2, 0.2), 0.05, 1.0)
    expert_ids_keys = jax.random.split(jax.random.fold_in(keys[4], 1), TOKENS // TOK_DEV)
    expert_ids_turns = jax.random.permutation(jax.random.fold_in(keys[4], 3), TOKENS // TOK_DEV)
    expert_ids = jax.vmap(lambda own, number: assign_block(jax.random.fold_in(keys[4], 2), own, number, TOK_DEV, EXPERTS, TOP, C_SRC, 2))(expert_ids_keys, expert_ids_turns).reshape((TOKENS, TOP))
    return {"hidden_act": hidden_act, "down_weight": down_weight, "out_grad": out_grad, "route_probs": route_probs, "expert_ids": expert_ids}


def keep_pairs(magnitude):
    first = magnitude[:, :, None, :]
    second = magnitude[:, None, :, :]
    lower = lax.broadcasted_iota(jnp.int32, (4, 4), 1) < lax.broadcasted_iota(jnp.int32, (4, 4), 0)
    beats = (second > first) | ((second == first) & lower[None, :, :, None])
    return jnp.sum(beats.astype(jnp.int32), axis=2) < 2


def row_pattern(weight):
    rows, cols = weight.shape
    return keep_pairs(jnp.abs(weight).reshape(rows // 4, 4, cols)).reshape(rows, cols)


def col_pattern(weight):
    rows, cols = weight.shape
    grouped = jnp.abs(weight).reshape(rows, cols // 4, 4).transpose(0, 2, 1)
    return keep_pairs(grouped).transpose(0, 2, 1).reshape(rows, cols)


def one_expert(items):
    hidden, weight, rows, probs = items
    row_kept = row_pattern(weight)
    col_kept = col_pattern(weight)
    weight_row = jnp.where(row_kept, weight, jnp.zeros_like(weight))
    weight_col = jnp.where(col_kept, weight, jnp.zeros_like(weight))
    scaled = (probs[:, None] * rows.astype(jnp.float32)).astype(jnp.bfloat16)
    hidden_grad = jnp.dot(scaled, weight_col.T, preferred_element_type=jnp.float32).astype(jnp.bfloat16)
    product = jnp.dot(hidden.T, scaled, preferred_element_type=jnp.float32)
    weight_grad = jnp.where(row_kept, product, jnp.zeros_like(product)).astype(jnp.bfloat16)
    back = jnp.dot(rows, weight_row.T, preferred_element_type=jnp.float32)
    score = jnp.sum(hidden.astype(jnp.float32) * back, axis=1)
    return weight_grad, hidden_grad, score


def reference(hidden_act, down_weight, out_grad, route_probs, expert_ids):
    blocks = TOKENS // TOK_DEV
    grouped = expert_ids.reshape(blocks, TOK_DEV * TOP)
    onehot = (grouped[:, :, None] == jnp.arange(EXPERTS, dtype=jnp.int32)[None, None, :]).astype(jnp.int32)
    rank = jnp.sum((jnp.cumsum(onehot, axis=1) - onehot) * onehot, axis=2)
    block_index = jnp.arange(blocks, dtype=jnp.int32)[:, None]
    slot = (block_index * C_SRC + rank).reshape(-1).astype(jnp.int32)
    expert = expert_ids.reshape(-1).astype(jnp.int32)
    token = (jnp.arange(TOKENS * TOP, dtype=jnp.int32) // TOP).astype(jnp.int32)
    rows = jnp.zeros((EXPERTS, CAP, D), out_grad.dtype).at[expert, slot].set(out_grad[token])
    probs = jnp.zeros((EXPERTS, CAP), route_probs.dtype).at[expert, slot].set(route_probs.reshape(-1))
    weight_grad, hidden_grad, score = lax.map(one_expert, (hidden_act, down_weight, rows, probs))
    prob_grad = score[expert, slot].reshape(TOKENS, TOP)
    return weight_grad, hidden_grad, prob_grad
```

```python
import jax
import jax.numpy as jnp
from jax import lax
from jax.experimental import pallas as pl
from jax.experimental.pallas import tpu as pltpu
from jax.sharding import PartitionSpec as P

BF = jnp.bfloat16
F32 = jnp.float32
MESH = pl.DeviceIdType.MESH

TOKENS = 128
TOP = 4
QUARTER = 720
WIDTH = 2880
CHUNK = 768
HALF = 384
META = 2 * CHUNK + 2 * CHUNK - 256
SLOT = 16
PLANES = 8
COLS = 4
PLANE = 8

SCHEDULE = (
    "A00", "A01", "M0", "A10", "A20", "C00", "C01", "M1", "A11", "A21", "M2", "C10",
    "C20", "A30", "A40", "C11", "C21", "M3", "A31", "A41", "D00", "D01", "C30", "C40",
    "M4", "A50", "A60", "C31", "C41", "A51", "A61", "M5", "D10", "D11", "C50", "C60",
    "A70", "A71", "C51", "C61", "G0", "C70", "C71", "K0", "K1", "K2", "D20", "D21",
    "D30", "D31", "G1", "K3", "K4", "K5", "K6", "K7", "D40", "D41", "D50", "D51",
    "G2", "D60", "D61", "D70", "D71", "G3",
)


def dot(a, b, ca, cb):
    return lax.dot_general(a, b, (((ca,), (cb,)), ((), ())), preferred_element_type=F32)


def iota(shape, dim):
    return lax.broadcasted_iota(jnp.int32, shape, dim)


def onehot(cond):
    return jnp.where(cond, 1.0, 0.0).astype(BF)


def keep(a0, a1, a2, a3):
    b01, b02, b03 = a0 >= a1, a0 >= a2, a0 >= a3
    b12, b13, b23 = a1 >= a2, a1 >= a3, a2 >= a3
    n01, n02, n03 = ~b01, ~b02, ~b03
    n12, n13, n23 = ~b12, ~b13, ~b23

    def two(a, b, c):
        return onehot((a & b) | (c & (a | b)))

    return two(b01, b02, b03), two(n01, b12, b13), two(n02, n12, b23), two(n03, n13, n23)


def kernel(
    ids_ref, probs_ref, og_ref, w_hbm, hid_hbm,
    wg_ref, hg_ref, pg_ref,
    nb, zb0, zb1, selb, dsel, fwd, bwd, up, down, rows, wv, wc, wr, rm, acc, hid, hsb, kmask, sc, etp_in, pln_in, zout, zin,
    nb_s, nb_r, z_s, z_r, p_s, p_r, l_s, y_s, y_r, s_s, s_r,
    r1_s, r1_r, r2_s, r2_r, r3_s, r3_r, w_sem, hid_sem,
):
    e = lax.axis_index("expert")
    q = lax.axis_index("etp")
    z = e // PLANE
    x = (e // 2) % COLS
    yh = e % 2
    ylo, core = q // 2, q % 2
    q1 = ylo * 2 + 1 - core
    q2 = (1 - ylo) * 2 + core
    q3 = (1 - ylo) * 2 + 1 - core
    pending = []

    def send(src, dst, ss, rs, dev):
        cp = pltpu.make_async_remote_copy(src, dst, ss, rs, device_id=dev, device_id_type=MESH)
        cp.start()
        pending.append(cp)

    def arrived(ref, sem):
        pltpu.make_async_copy(ref, ref, sem).wait()

    def zdev(d):
        return (((z + d) % PLANES) * PLANE + e % PLANE, q)

    def rel(i):
        return -((i + 1) // 2) if i % 2 else i // 2

    rels = [(dx, dy) for dy in range(2) for dx in range(COLS) if (dx, dy) != (0, 0)]

    def plane_to(dx, dy):
        ex = z * PLANE + ((x + dx) % COLS) * 2 + (yh if dy == 0 else 1 - yh)
        return (ex, q if dy == 0 else q2)

    w_cp = pltpu.make_async_copy(w_hbm, wv, w_sem)
    w_cp.start()
    hid_cp = []
    for i in range(PLANES):
        src = (z + rel(i) + PLANES) % PLANES
        cp = pltpu.make_async_copy(
            hid_hbm.at[:, pl.ds(pl.multiple_of(src * 128, 128), 128)],
            hid.at[:, pl.ds(i * 128, 128)], hid_sem.at[i])
        cp.start()
        hid_cp.append(cp)

    peers = [zdev(d) for d in range(1, PLANES)]
    peers += [plane_to(dx, dy) for dx, dy in rels]
    peers += [(e, (q + d) % 4) for d in range(1, 4)]
    barrier = pltpu.get_barrier_semaphore()
    for dev in peers:
        pl.semaphore_signal(barrier, inc=1, device_id=dev, device_id_type=MESH)
    lane = iota((128, 128), 1)
    sub = iota((128, 128), 0)
    eye = lane == sub
    before = onehot(sub < lane)
    sub_expert = (sub // SLOT).astype(F32)
    sub_rank = (sub % SLOT).astype(F32)

    def column(r):
        return jnp.sum(jnp.where(eye, r, 0.0), axis=1, keepdims=True)

    def as_row(c):
        return jnp.sum(jnp.where(eye, c, 0.0), axis=0, keepdims=True)

    def routes(ids, plane):
        ex = sub_expert + (plane * PLANE).astype(F32)
        eqs = [ids[k:k + 1, :] == ex for k in range(TOP)]
        any_k = eqs[0] | eqs[1] | eqs[2] | eqs[3]
        rank = dot(onehot(any_k), before, 1, 0)
        return eqs, any_k, rank == sub_rank

    ids_f = ids_ref[...].astype(F32)
    diff = iota((QUARTER, HALF), 0) - iota((QUARTER, HALF), 1)
    zb0[0, 0:128, :] = dot(og_ref[...], onehot(diff == 48 * q), 0, 0).astype(BF)
    zb0[0, 128:144, 0:128] = jnp.concatenate([ids_f, jnp.zeros((12, 128), F32)], axis=0).astype(BF)
    zb0[0, 128:144, 128:HALF] = jnp.zeros((16, HALF - 128), BF)
    pl.semaphore_wait(barrier, len(peers))

    def zsend(src, i, h, d):
        buf = zb1 if h else zb0
        send(buf.at[src], buf.at[i], z_s.at[i, h], z_r.at[i, h], zdev(d % PLANES))

    send(og_ref.at[pl.ds(0, 144), :], nb, nb_s, nb_r, (e, (q + 3) % 4))
    zsend(0, 1, 0, 1)
    zsend(0, 2, 0, -1)

    probs = probs_ref[...]
    own_ids = [column(ids_f[k:k + 1, :]) for k in range(TOP)]
    own_probs = [column(probs[k:k + 1, :]) for k in range(TOP)]

    def meta(off):
        out = jnp.zeros((128, 128), F32)
        for k in range(TOP):
            hi = own_probs[k].astype(BF).astype(F32)
            rest = own_probs[k] - hi
            mid = rest.astype(BF).astype(F32)
            lo = rest - mid
            for part, v in enumerate((own_ids[k], hi, mid, lo)):
                out = out + jnp.where(lane == off + 4 * part + k, v, 0.0)
        return out

    def step_second():
        chunk = dot(og_ref[...], onehot(diff == 48 * q + HALF), 0, 0)
        last = jnp.where(q == 3, 1.0, 0.0)
        tile = last * meta(64)
        arrived(nb, nb_r)
        gap = jnp.where(q < 3, 48 * q - QUARTER + HALF, 100000)
        chunk = chunk + dot(nb[...], onehot(diff[:144] == gap), 0, 0)
        zb1[0] = chunk.astype(BF)
        zb1[0, :, 128:256] = (chunk[:, 128:256] + tile).astype(BF)
        zsend(0, 1, 1, 1)
        zsend(0, 2, 1, -1)

    def lanes_of(qq, h):
        return pl.ds(pl.multiple_of(qq * CHUNK + h * HALF, 128), HALF)

    def step_a(i, h):
        buf = zb1 if h else zb0
        if i == 0 and h == 1:
            step_second()
        if i > 0:
            arrived(buf.at[i], z_r.at[i, h])
            if i in (1, 3) or (i, h) == (5, 0):
                zsend(i, i + 2, h, 1)
            if i in (2, 4):
                zsend(i, i + 2, h, -1)
            if (i, h) == (6, 1):
                zsend(i, 7, h, -1)
        if h == 0:
            _, any_k, hit = routes(zb0[i, 128:144, 0:128].astype(F32), z)
            dsel[i] = onehot(any_k & hit)
        picked = dot(dsel[i], buf[i, 0:128, :], 1, 0)
        selb[i, h] = picked.astype(BF).reshape(COLS, 2, SLOT, HALF)
        for dx, dy in rels:
            xt = (x + dx) % COLS
            yt = yh if dy == 0 else 1 - yh
            at = dy * COLS + dx
            send(selb.at[i, h, xt, yt], rows.at[i, x, yh, :, lanes_of(q, h)],
                 p_s.at[i, h, at], p_r.at[i, h, at], plane_to(dx, dy))
        pltpu.make_async_copy(
            selb.at[i, h, x, yh], rows.at[i, x, yh, :, lanes_of(q, h)], l_s.at[i, h]).start()

    def half(i, y, qq, h):
        return rows.at[i, :, y, :, lanes_of(qq, h)]

    def step_c(i, h):
        arrived(selb.at[i, h, 0, 0], l_s.at[i, h])
        for dx, dy in rels:
            xs = (x - dx + COLS) % COLS
            ys = yh if dy == 0 else 1 - yh
            qs = q if dy == 0 else q2
            arrived(rows.at[i, xs, ys, :, lanes_of(qs, h)], p_r.at[i, h, dy * COLS + dx])
        one, two = half(i, yh, q, h), half(i, 1 - yh, q2, h)
        send(one, one, y_s.at[i, h, 0], y_r.at[i, h, 0], (e, q2))
        send(two, two, y_s.at[i, h, 1], y_r.at[i, h, 1], (e, q2))
        send(one, one, s_s.at[i, h, 0], s_r.at[i, h, 0], (e, q1))
        send(two, two, s_s.at[i, h, 1], s_r.at[i, h, 1], (e, q1))

    def step_d(i, h):
        one, two = half(i, yh, q2, h), half(i, 1 - yh, q, h)
        arrived(one, y_r.at[i, h, 0])
        send(one, one, s_s.at[i, h, 2], s_r.at[i, h, 2], (e, q1))
        arrived(two, y_r.at[i, h, 1])
        send(two, two, s_s.at[i, h, 3], s_r.at[i, h, 3], (e, q1))

    def tables():
        f, c = iota((512, 512), 0), iota((512, 512), 1)
        fwd[...] = onehot((c % 128 == f // 4) & (c // 128 == f % 4))
        c, f = iota((512, 512), 0), iota((512, 512), 1)
        bwd[...] = onehot((c % 128 == f // 4) & (c // 128 == f % 4))
        c, f = iota((256, 240), 0), iota((256, 240), 1)
        up[...] = onehot((c % 64 == f // 4) & (c // 64 == f % 4))
        f, c = iota((240, 256), 0), iota((240, 256), 1)
        down[...] = onehot((c % 64 == f // 4) & (c // 64 == f % 4))

    def step_m(b):
        if b == 0:
            tables()
            w_cp.wait()
        lo = 512 * b
        n = min(512, WIDTH - lo)
        wb = wv[:, lo:lo + n]
        a = jnp.abs(dot(wb, fwd[0:n, :], 1, 0)).astype(BF)
        kept = jnp.concatenate(keep(*[a[:, 128 * p:128 * p + 128] for p in range(4)]), axis=1)
        wc[:, lo:lo + n] = wb * dot(kept, bwd[:, 0:n], 1, 0).astype(BF)
        for m in range(3):
            part = wb[240 * m:240 * m + 240]
            a = jnp.abs(dot(up[...], part, 1, 0)).astype(BF)
            kept = jnp.concatenate(keep(*[a[64 * p:64 * p + 64] for p in range(4)]), axis=0)
            mask = dot(down[...], kept, 1, 0).astype(BF)
            rm[240 * m:240 * m + 240, lo:lo + n] = mask
            wr[240 * m:240 * m + 240, lo:lo + n] = part * mask

    def step_k(i):
        eqs, _, hit = routes(ids_f, (z - rel(i) + PLANES) % PLANES)
        for k in range(TOP):
            kmask[i, k] = jnp.where(eqs[k] & hit, 1.0, 0.0)

    def step_g(g):
        for i in (2 * g, 2 * g + 1):
            for h in range(2):
                arrived(half(i, yh, q1, h), s_r.at[i, h, 0])
                arrived(half(i, 1 - yh, q3, h), s_r.at[i, h, 1])
                arrived(half(i, yh, q3, h), s_r.at[i, h, 2])
                arrived(half(i, 1 - yh, q1, h), s_r.at[i, h, 3])
            hid_cp[i].wait()
        span = pl.ds(256 * g, 256)

        def r(lo, n):
            return rows[2 * g:2 * g + 2, :, :, :, lo:lo + n].reshape(256, n)

        back = dot(wr[...], r(0, WIDTH), 1, 1)
        score = jnp.sum(hid[:, span].astype(F32) * back, axis=0, keepdims=True)
        sc[2 * g:2 * g + 1, :] = score[:, :128]
        sc[2 * g + 1:2 * g + 2, :] = score[:, 128:]
        if g == 3:
            return_one()
        mt = r(META, 128).astype(F32)
        total = pltpu.roll(mt, 124, 1) + pltpu.roll(mt, 120, 1) + pltpu.roll(mt, 116, 1)
        wide = iota((256, 128), 1)
        mine = (wide >= 64) & (wide < 68) & (mt == e.astype(F32))
        pc = jnp.sum(jnp.where(mine, total, 0.0), axis=1, keepdims=True)
        pr = jnp.concatenate([as_row(pc[:128]), as_row(pc[128:])], axis=1)
        grad = (dot(wc[...], r(0, WIDTH), 1, 1) * pr).astype(BF)
        for i in (2 * g, 2 * g + 1):
            src = (z + rel(i) + PLANES) % PLANES
            part = 128 * (i % 2)
            hg_ref[:, pl.ds(pl.multiple_of(src * 128, 128), 128)] = grad[:, part:part + 128]
        hsb[...] = (hid[:, span].astype(F32) * pr).astype(BF)
        if g == 3:
            return_two()
        if g < 3:
            for c in range(4):
                n = min(CHUNK, WIDTH - CHUNK * c)
                part = dot(hsb[...], r(CHUNK * c, n), 1, 0)
                if g > 0:
                    part = part + acc[:, CHUNK * c:CHUNK * c + n]
                acc[:, CHUNK * c:CHUNK * c + n] = part
        else:
            for m in range(3):
                at = slice(240 * m, 240 * m + 240)
                for c in range(4):
                    n = min(CHUNK, WIDTH - CHUNK * c)
                    ln = slice(CHUNK * c, CHUNK * c + n)
                    part = dot(hsb[at, :], r(CHUNK * c, n), 1, 0) + acc[at, ln]
                    wg_ref[at, ln] = jnp.where(rm[at, ln].astype(F32) > 0.5, part, 0.0).astype(BF)
                if m == 0:
                    return_three()

    def return_one():
        etp_in[q] = sc[...]
        for d in range(1, 4):
            send(etp_in.at[q], etp_in.at[q], r1_s.at[d], r1_r.at[d], (e, (q + d) % 4))

    def return_two():
        for d in range(1, 4):
            arrived(etp_in.at[(q - d + 4) % 4], r1_r.at[d])
        sc[...] = (etp_in[0] + etp_in[1]) + (etp_in[2] + etp_in[3])
        for dx, dy in rels:
            send(sc, pln_in.at[dy * COLS + dx], r2_s.at[dy * COLS + dx],
                 r2_r.at[dy * COLS + dx], plane_to(dx, dy))

    def return_three():
        lane8 = iota((8, 128), 1) // SLOT
        own = 2 * x + yh
        v = jnp.where(lane8 == own, sc[...], 0.0)
        for dx, dy in rels:
            arrived(pln_in.at[dy * COLS + dx], r2_r.at[dy * COLS + dx])
            sb = 2 * ((x - dx + COLS) % COLS) + (yh if dy == 0 else 1 - yh)
            shifted = pltpu.roll(pln_in[dy * COLS + dx], ((sb - own + PLANE) % PLANE) * SLOT, 1)
            v = v + jnp.where(lane8 == sb, shifted, 0.0)
        zout[...] = v
        for i in range(1, PLANES):
            send(zout, zin.at[i], r3_s.at[i], r3_r.at[i], zdev((rel(i) + PLANES) % PLANES))

    def return_four():
        totals = [jnp.zeros((128, 128), F32) for _ in range(TOP)]
        for i in range(PLANES):
            if i == 0:
                v = column(zout[0:1, :])
            else:
                arrived(zin.at[i], r3_r.at[i])
                v = column(zin[i, i:i + 1, :])
            for k in range(TOP):
                totals[k] = totals[k] + kmask[i, k] * v
        for k in range(TOP):
            pg_ref[k:k + 1, :] = jnp.sum(totals[k], axis=0, keepdims=True)

    steps = {"A": step_a, "C": step_c, "D": step_d, "M": step_m, "K": step_k, "G": step_g}
    for item in SCHEDULE:
        steps[item[0]](*[int(c) for c in item[1:]])
    return_four()
    for cp in pending:
        cp.wait_send()


def call(ids, probs, og, weight, hidden):
    hbm = pl.BlockSpec(memory_space=pltpu.HBM)
    out = pl.BlockSpec(memory_space=pltpu.VMEM)
    vmem = pl.BlockSpec(memory_space=pltpu.VMEM)
    dma = pltpu.SemaphoreType.DMA
    return pl.pallas_call(
        kernel,
        out_shape=(
            pltpu.VMEM((QUARTER, WIDTH), BF),
            pltpu.VMEM((QUARTER, 1024), BF),
            jax.ShapeDtypeStruct((TOP, TOKENS), F32),
        ),
        in_specs=[vmem, vmem, vmem, hbm, hbm],
        out_specs=(out, out, vmem),
        scratch_shapes=[
            pltpu.VMEM((144, TOKENS), BF),
            pltpu.VMEM((8, TOKENS + 16, HALF), BF),
            pltpu.VMEM((8, TOKENS, HALF), BF),
            pltpu.VMEM((8, 2, COLS, 2, SLOT, HALF), BF),
            pltpu.VMEM((8, 128, 128), BF),
            pltpu.VMEM((512, 512), BF),
            pltpu.VMEM((512, 512), BF),
            pltpu.VMEM((256, 240), BF),
            pltpu.VMEM((240, 256), BF),
            pltpu.VMEM((8, COLS, 2, SLOT, 4 * CHUNK), BF),
            pltpu.VMEM((QUARTER, WIDTH), BF),
            pltpu.VMEM((QUARTER, WIDTH), BF),
            pltpu.VMEM((QUARTER, WIDTH), BF),
            pltpu.VMEM((QUARTER, WIDTH), BF),
            pltpu.VMEM((QUARTER, WIDTH), F32),
            pltpu.VMEM((QUARTER, 1024), BF),
                pltpu.VMEM((QUARTER, 256), BF),
            pltpu.VMEM((8, TOP, 128, 128), F32),
            pltpu.VMEM((8, 128), F32),
            pltpu.VMEM((4, 8, 128), F32),
            pltpu.VMEM((8, 8, 128), F32),
            pltpu.VMEM((8, 128), F32),
            pltpu.VMEM((8, 8, 128), F32),
            dma, dma, dma((8, 2)), dma((8, 2)), dma((8, 2, 8)), dma((8, 2, 8)), dma((8, 2)),
            dma((8, 2, 2)), dma((8, 2, 2)), dma((8, 2, 4)), dma((8, 2, 4)),
            dma((4,)), dma((4,)), dma((8,)), dma((8,)), dma((8,)), dma((8,)),
            dma, dma((8,)),
        ],
        compiler_params=pltpu.CompilerParams(
            collective_id=0, has_side_effects=True, vmem_limit_bytes=50 * 1024 * 1024),
        cost_estimate=pl.CostEstimate(
            flops=3 * 2 * 1024 * 720 * 2880, bytes_accessed=20_000_000, transcendentals=0),
    )(ids, probs, og, weight, hidden)


def local(hidden_act, down_weight, out_grad, route_probs, expert_ids):
    wg, hg, pg = call(
        expert_ids.T, route_probs.T, out_grad.T, down_weight[0], hidden_act[0].T)
    return wg[None], hg.T[None], pg.T


def solution(mesh):
    return jax.shard_map(
        local,
        mesh=mesh,
        in_specs=(
            P("expert", None, "etp"),
            P("expert", "etp", None),
            P("expert", "etp"),
            P("expert", None),
            P("expert", None),
        ),
        out_specs=(P("expert", "etp", None), P("expert", None, "etp"), P("expert", None)),
        check_vma=False,
    )
```

```python
import jax
import jax.numpy as jnp
from jax import lax
from jax.experimental import pallas as pl
from jax.experimental.pallas import tpu as pltpu
from jax.sharding import PartitionSpec as P

BF = jnp.bfloat16
F32 = jnp.float32
MESH = pl.DeviceIdType.MESH

TOKENS = 128
TOP = 4
QUARTER = 720
WIDTH = 2880
CHUNK = 768
LATE = 512
EARLY = 256
META = 2 * CHUNK + 2 * CHUNK - 256
SLOT = 16
PLANES = 8
COLS = 4
PLANE = 8

SCHEDULE = (
    "A00", "M0", "A01", "A02", "C00", "A10", "A20", "M1", "C01", "C02", "A11", "A21",
    "A12", "A22", "C10", "C20", "M2", "A30", "A40", "C11", "C21", "C12", "C22", "A31",
    "A41", "A32", "A42", "D0", "M3", "C30", "C40", "A50", "A60", "C31", "C41", "C32",
    "C42", "A51", "A61", "A52", "A62", "D1", "M4", "C50", "C60", "A70", "A71", "A72",
    "C51", "C61", "C52", "C62", "M5", "C70", "C71", "C72", "D2", "K0", "K1", "K2",
    "K3", "B0", "W0", "D3", "D4", "B1", "W1", "K4", "K5", "K6", "K7", "D5",
    "D6", "B2", "D7", "B3", "R1", "W2", "H1", "R2", "W3", "H2", "R3", "H3",
    "H0", "R4",
)


def dot(a, b, ca, cb):
    return lax.dot_general(a, b, (((ca,), (cb,)), ((), ())), preferred_element_type=F32)


def iota(shape, dim):
    return lax.broadcasted_iota(jnp.int32, shape, dim)


def onehot(cond):
    return jnp.where(cond, 1.0, 0.0).astype(BF)


def keep(a0, a1, a2, a3):
    b01, b02, b03 = a0 >= a1, a0 >= a2, a0 >= a3
    b12, b13, b23 = a1 >= a2, a1 >= a3, a2 >= a3
    n01, n02, n03 = ~b01, ~b02, ~b03
    n12, n13, n23 = ~b12, ~b13, ~b23

    def two(a, b, c):
        return onehot((a & b) | (c & (a | b)))

    return two(b01, b02, b03), two(n01, b12, b13), two(n02, n12, b23), two(n03, n13, n23)


def kernel(
    ids_ref, probs_ref, og_ref, w_hbm, hid_hbm,
    wg_ref, hg_ref, pg_ref,
    nb, zb0, zb1, zb2, sb0, sb1, sb2, dsel, fwd, bwd, up, down, rows, wv, wc, wr, rm, acc, hid, hsb, prs, kmask, sc, etp_in, pln_in, zout, zin,
    nb_s, nb_r, x_s, x_r, z_s, z_r, p_s, p_r, l_s, y_s, y_r, s_s, s_r,
    r1_s, r1_r, r2_s, r2_r, r3_s, r3_r, w_sem, hid_sem,
):
    e = lax.axis_index("expert")
    q = lax.axis_index("etp")
    z = e // PLANE
    x = (e // 2) % COLS
    yh = e % 2
    ylo, core = q // 2, q % 2
    q1 = ylo * 2 + 1 - core
    q2 = (1 - ylo) * 2 + core
    q3 = (1 - ylo) * 2 + 1 - core
    pending = []

    def send(src, dst, ss, rs, dev):
        cp = pltpu.make_async_remote_copy(src, dst, ss, rs, device_id=dev, device_id_type=MESH)
        cp.start()
        pending.append(cp)

    def arrived(ref, sem):
        pltpu.make_async_copy(ref, ref, sem).wait()

    def zdev(d):
        return (((z + d) % PLANES) * PLANE + e % PLANE, q)

    def rel(i):
        return -((i + 1) // 2) if i % 2 else i // 2

    rels = [(dx, dy) for dy in range(2) for dx in range(COLS) if (dx, dy) != (0, 0)]

    def plane_to(dx, dy):
        ex = z * PLANE + ((x + dx) % COLS) * 2 + (yh if dy == 0 else 1 - yh)
        return (ex, q if dy == 0 else q2)

    w_cp = pltpu.make_async_copy(w_hbm, wv, w_sem)
    w_cp.start()
    hid_cp = []
    for i in range(PLANES):
        src = (z + rel(i) + PLANES) % PLANES
        cp = pltpu.make_async_copy(
            hid_hbm.at[:, pl.ds(pl.multiple_of(src * 128, 128), 128)],
            hid.at[:, pl.ds(i * 128, 128)], hid_sem.at[i])
        cp.start()
        hid_cp.append(cp)

    peers = [zdev(d) for d in range(1, PLANES)]
    peers += [plane_to(dx, dy) for dx, dy in rels]
    peers += [(e, (q + d) % 4) for d in range(1, 4)]
    barrier = pltpu.get_barrier_semaphore()
    for dev in peers:
        pl.semaphore_signal(barrier, inc=1, device_id=dev, device_id_type=MESH)
    lane = iota((128, 128), 1)
    sub = iota((128, 128), 0)
    eye = lane == sub
    before = onehot(sub < lane)
    sub_expert = (sub // SLOT).astype(F32)
    sub_rank = (sub % SLOT).astype(F32)

    def column(r):
        return jnp.sum(jnp.where(eye, r, 0.0), axis=1, keepdims=True)

    def as_row(c):
        return jnp.sum(jnp.where(eye, c, 0.0), axis=0, keepdims=True)

    def routes(ids, plane):
        ex = sub_expert + (plane * PLANE).astype(F32)
        eqs = [ids[k:k + 1, :] == ex for k in range(TOP)]
        any_k = eqs[0] | eqs[1] | eqs[2] | eqs[3]
        rank = dot(onehot(any_k), before, 1, 0)
        return eqs, any_k, rank == sub_rank

    ids_f = ids_ref[...].astype(F32)
    diff = iota((QUARTER, LATE), 0) - iota((QUARTER, LATE), 1)
    zb0[0, 0:128, :] = dot(og_ref[...], onehot(diff == 48 * q), 0, 0).astype(BF)
    zb0[0, 128:144, 0:128] = jnp.concatenate([ids_f, jnp.zeros((12, 128), F32)], axis=0).astype(BF)
    zb0[0, 128:144, 128:LATE] = jnp.zeros((16, LATE - 128), BF)
    pl.semaphore_wait(barrier, len(peers))

    zbs, sbs = (zb0, zb1, zb2), (sb0, sb1, sb2)

    def zsend(src, i, h, d):
        buf = zbs[h]
        send(buf.at[src], buf.at[i], z_s.at[i, h], z_r.at[i, h], zdev(d % PLANES))

    send(og_ref.at[pl.ds(0, 144), :], nb, nb_s, nb_r, (e, (q + 3) % 4))
    zsend(0, 1, 0, 1)
    zsend(0, 2, 0, -1)

    probs = probs_ref[...]
    own_ids = [column(ids_f[k:k + 1, :]) for k in range(TOP)]
    own_probs = [column(probs[k:k + 1, :]) for k in range(TOP)]

    def meta(off):
        out = jnp.zeros((128, 128), F32)
        for k in range(TOP):
            hi = own_probs[k].astype(BF).astype(F32)
            rest = own_probs[k] - hi
            mid = rest.astype(BF).astype(F32)
            lo = rest - mid
            for part, v in enumerate((own_ids[k], hi, mid, lo)):
                out = out + jnp.where(lane == off + 4 * part + k, v, 0.0)
        return out

    def step_second():
        diff = iota((QUARTER, EARLY), 0) - iota((QUARTER, EARLY), 1)
        chunk = dot(og_ref[...], onehot(diff == 48 * q + LATE), 0, 0)
        last = jnp.where(q == 3, 1.0, 0.0)
        tile = last * meta(64)
        arrived(nb, nb_r)
        gap = jnp.where(q < 3, 48 * q - QUARTER + LATE, 100000)
        chunk = chunk + dot(nb[...], onehot(diff[:144] == gap), 0, 0)
        zb1[0] = jnp.concatenate([chunk[:, 0:128] + tile, chunk[:, 128:256]], axis=1).astype(BF)
        send(zb1.at[0], zb2.at[0], x_s, x_r, (e, q2))
        zsend(0, 1, 1, 1)
        zsend(0, 2, 1, -1)

    def lanes_of(qq, h):
        if h == 0:
            return pl.ds(pl.multiple_of(qq * CHUNK, 128), LATE)
        return pl.ds(pl.multiple_of(qq * CHUNK + LATE, 128), EARLY)

    def step_a(i, h):
        buf, out = zbs[h], sbs[h]
        if i == 0 and h == 1:
            step_second()
        if i == 0 and h == 2:
            arrived(zb2.at[0], x_r)
            zsend(0, 1, 2, 1)
            zsend(0, 2, 2, -1)
        if i > 0:
            arrived(buf.at[i], z_r.at[i, h])
            if i in (1, 3) or (i == 5 and h == 0):
                zsend(i, i + 2, h, 1)
            if i in (2, 4):
                zsend(i, i + 2, h, -1)
            if i == 6 and h > 0:
                zsend(i, 7, h, -1)
        if h == 0:
            _, any_k, hit = routes(zb0[i, 128:144, 0:128].astype(F32), z)
            dsel[i] = onehot(any_k & hit)
        picked = dot(dsel[i], buf[i, 0:128, :], 1, 0)
        out[i] = picked.astype(BF).reshape(COLS, 2, SLOT, LATE if h == 0 else EARLY)
        lanes = lanes_of(q2 if h == 2 else q, h)
        for dx, dy in rels:
            xt = (x + dx) % COLS
            yt = yh if dy == 0 else 1 - yh
            at = dy * COLS + dx
            send(out.at[i, xt, yt], rows.at[i, x, yh, :, lanes],
                 p_s.at[i, h, at], p_r.at[i, h, at], plane_to(dx, dy))
        pltpu.make_async_copy(
            out.at[i, x, yh], rows.at[i, x, yh, :, lanes], l_s.at[i, h]).start()

    def part(i, y, qq, h):
        return rows.at[i, :, y, :, lanes_of(qq, h)]

    def step_c(i, h):
        arrived(sbs[h].at[i, 0, 0], l_s.at[i, h])
        qa, qb = (q2, q) if h == 2 else (q, q2)
        for dx, dy in rels:
            xs = (x - dx + COLS) % COLS
            ys = yh if dy == 0 else 1 - yh
            qs = qa if dy == 0 else qb
            arrived(rows.at[i, xs, ys, :, lanes_of(qs, h)], p_r.at[i, h, dy * COLS + dx])
        one, two = part(i, yh, qa, h), part(i, 1 - yh, qb, h)
        if h == 0:
            send(one, one, y_s.at[i, 0], y_r.at[i, 0], (e, q2))
            send(two, two, y_s.at[i, 1], y_r.at[i, 1], (e, q2))
        send(one, one, s_s.at[i, h, 0], s_r.at[i, h, 0], (e, q1))
        send(two, two, s_s.at[i, h, 1], s_r.at[i, h, 1], (e, q1))

    def step_d(i):
        one, two = part(i, yh, q2, 0), part(i, 1 - yh, q, 0)
        arrived(one, y_r.at[i, 0])
        send(one, one, s_s.at[i, 0, 2], s_r.at[i, 0, 2], (e, q1))
        arrived(two, y_r.at[i, 1])
        send(two, two, s_s.at[i, 0, 3], s_r.at[i, 0, 3], (e, q1))

    def tables():
        f, c = iota((512, 512), 0), iota((512, 512), 1)
        fwd[...] = onehot((c % 128 == f // 4) & (c // 128 == f % 4))
        c, f = iota((512, 512), 0), iota((512, 512), 1)
        bwd[...] = onehot((c % 128 == f // 4) & (c // 128 == f % 4))
        c, f = iota((256, 240), 0), iota((256, 240), 1)
        up[...] = onehot((c % 64 == f // 4) & (c // 64 == f % 4))
        f, c = iota((240, 256), 0), iota((240, 256), 1)
        down[...] = onehot((c % 64 == f // 4) & (c // 64 == f % 4))

    def step_m(b):
        if b == 0:
            tables()
            w_cp.wait()
        lo = 512 * b
        n = min(512, WIDTH - lo)
        wb = wv[:, lo:lo + n]
        a = jnp.abs(dot(wb, fwd[0:n, :], 1, 0)).astype(BF)
        kept = jnp.concatenate(keep(*[a[:, 128 * p:128 * p + 128] for p in range(4)]), axis=1)
        wc[:, lo:lo + n] = wb * dot(kept, bwd[:, 0:n], 1, 0).astype(BF)
        for m in range(3):
            part = wb[240 * m:240 * m + 240]
            a = jnp.abs(dot(up[...], part, 1, 0)).astype(BF)
            kept = jnp.concatenate(keep(*[a[64 * p:64 * p + 64] for p in range(4)]), axis=0)
            mask = dot(down[...], kept, 1, 0).astype(BF)
            rm[240 * m:240 * m + 240, lo:lo + n] = mask
            wr[240 * m:240 * m + 240, lo:lo + n] = part * mask

    def step_k(i):
        eqs, _, hit = routes(ids_f, (z - rel(i) + PLANES) % PLANES)
        for k in range(TOP):
            kmask[i, k] = jnp.where(eqs[k] & hit, 1.0, 0.0)

    def r(g, lo, n):
        return rows[2 * g:2 * g + 2, :, :, :, lo:lo + n].reshape(256, n)

    def span(g):
        return slice(256 * g, 256 * g + 256)

    def step_b(g):
        for i in (2 * g, 2 * g + 1):
            arrived(part(i, yh, q1, 0), s_r.at[i, 0, 0])
            arrived(part(i, 1 - yh, q3, 0), s_r.at[i, 0, 1])
            arrived(part(i, yh, q3, 0), s_r.at[i, 0, 2])
            arrived(part(i, 1 - yh, q1, 0), s_r.at[i, 0, 3])
            arrived(part(i, yh, q1, 1), s_r.at[i, 1, 0])
            arrived(part(i, 1 - yh, q3, 1), s_r.at[i, 1, 1])
            arrived(part(i, yh, q3, 2), s_r.at[i, 2, 0])
            arrived(part(i, 1 - yh, q1, 2), s_r.at[i, 2, 1])
            hid_cp[i].wait()
        back = dot(wr[...], r(g, 0, WIDTH), 1, 1)
        score = jnp.sum(hid[:, span(g)].astype(F32) * back, axis=0, keepdims=True)
        sc[2 * g:2 * g + 1, :] = score[:, :128]
        sc[2 * g + 1:2 * g + 2, :] = score[:, 128:]

    def step_w(g):
        mt = r(g, META, 128).astype(F32)
        total = pltpu.roll(mt, 124, 1) + pltpu.roll(mt, 120, 1) + pltpu.roll(mt, 116, 1)
        wide = iota((256, 128), 1)
        mine = (wide >= 64) & (wide < 68) & (mt == e.astype(F32))
        pc = jnp.sum(jnp.where(mine, total, 0.0), axis=1, keepdims=True)
        pr = jnp.concatenate([as_row(pc[:128]), as_row(pc[128:])], axis=1)
        prs[:, span(g)] = pr
        hsb[:, span(g)] = (hid[:, span(g)].astype(F32) * pr).astype(BF)
        for c in range(4):
            n = min(CHUNK, WIDTH - CHUNK * c)
            ln = slice(CHUNK * c, CHUNK * c + n)
            share = dot(hsb[:, span(g)], r(g, CHUNK * c, n), 1, 0)
            if g > 0:
                share = share + acc[:, ln]
            if g < 3:
                acc[:, ln] = share
            else:
                wg_ref[:, ln] = jnp.where(rm[:, ln].astype(F32) > 0.5, share, 0.0).astype(BF)

    def step_h(g):
        grad = (dot(wc[...], r(g, 0, WIDTH), 1, 1) * prs[:, span(g)]).astype(BF)
        for i in (2 * g, 2 * g + 1):
            src = (z + rel(i) + PLANES) % PLANES
            at = 128 * (i % 2)
            hg_ref[:, pl.ds(pl.multiple_of(src * 128, 128), 128)] = grad[:, at:at + 128]

    def return_one():
        etp_in[q] = sc[...]
        for d in range(1, 4):
            send(etp_in.at[q], etp_in.at[q], r1_s.at[d], r1_r.at[d], (e, (q + d) % 4))

    def return_two():
        for d in range(1, 4):
            arrived(etp_in.at[(q - d + 4) % 4], r1_r.at[d])
        sc[...] = (etp_in[0] + etp_in[1]) + (etp_in[2] + etp_in[3])
        for dx, dy in rels:
            send(sc, pln_in.at[dy * COLS + dx], r2_s.at[dy * COLS + dx],
                 r2_r.at[dy * COLS + dx], plane_to(dx, dy))

    def return_three():
        lane8 = iota((8, 128), 1) // SLOT
        own = 2 * x + yh
        v = jnp.where(lane8 == own, sc[...], 0.0)
        for dx, dy in rels:
            arrived(pln_in.at[dy * COLS + dx], r2_r.at[dy * COLS + dx])
            sb = 2 * ((x - dx + COLS) % COLS) + (yh if dy == 0 else 1 - yh)
            shifted = pltpu.roll(pln_in[dy * COLS + dx], ((sb - own + PLANE) % PLANE) * SLOT, 1)
            v = v + jnp.where(lane8 == sb, shifted, 0.0)
        zout[...] = v
        for i in range(1, PLANES):
            send(zout, zin.at[i], r3_s.at[i], r3_r.at[i], zdev((rel(i) + PLANES) % PLANES))

    def return_four():
        totals = [jnp.zeros((128, 128), F32) for _ in range(TOP)]
        for i in range(PLANES):
            if i == 0:
                v = column(zout[0:1, :])
            else:
                arrived(zin.at[i], r3_r.at[i])
                v = column(zin[i, i:i + 1, :])
            for k in range(TOP):
                totals[k] = totals[k] + kmask[i, k] * v
        for k in range(TOP):
            pg_ref[k:k + 1, :] = jnp.sum(totals[k], axis=0, keepdims=True)

    steps = {"A": step_a, "C": step_c, "D": step_d, "M": step_m, "K": step_k, "B": step_b, "W": step_w, "H": step_h,
             "R": lambda n: (return_one, return_two, return_three, return_four)[n - 1]()}
    for item in SCHEDULE:
        steps[item[0]](*[int(c) for c in item[1:]])
    for cp in pending:
        cp.wait_send()


def call(ids, probs, og, weight, hidden):
    hbm = pl.BlockSpec(memory_space=pltpu.HBM)
    out = pl.BlockSpec(memory_space=pltpu.VMEM)
    vmem = pl.BlockSpec(memory_space=pltpu.VMEM)
    dma = pltpu.SemaphoreType.DMA
    return pl.pallas_call(
        kernel,
        out_shape=(
            pltpu.VMEM((QUARTER, WIDTH), BF),
            pltpu.VMEM((QUARTER, 1024), BF),
            jax.ShapeDtypeStruct((TOP, TOKENS), F32),
        ),
        in_specs=[vmem, vmem, vmem, hbm, hbm],
        out_specs=(out, out, vmem),
        scratch_shapes=[
            pltpu.VMEM((144, TOKENS), BF),
            pltpu.VMEM((8, TOKENS + 16, LATE), BF),
            pltpu.VMEM((8, TOKENS, EARLY), BF),
            pltpu.VMEM((8, TOKENS, EARLY), BF),
            pltpu.VMEM((8, COLS, 2, SLOT, LATE), BF),
            pltpu.VMEM((8, COLS, 2, SLOT, EARLY), BF),
            pltpu.VMEM((8, COLS, 2, SLOT, EARLY), BF),
            pltpu.VMEM((8, 128, 128), BF),
            pltpu.VMEM((512, 512), BF),
            pltpu.VMEM((512, 512), BF),
            pltpu.VMEM((256, 240), BF),
            pltpu.VMEM((240, 256), BF),
            pltpu.VMEM((8, COLS, 2, SLOT, 4 * CHUNK), BF),
            pltpu.VMEM((QUARTER, WIDTH), BF),
            pltpu.VMEM((QUARTER, WIDTH), BF),
            pltpu.VMEM((QUARTER, WIDTH), BF),
            pltpu.VMEM((QUARTER, WIDTH), BF),
            pltpu.VMEM((QUARTER, WIDTH), F32),
            pltpu.VMEM((QUARTER, 1024), BF),
                pltpu.VMEM((QUARTER, 1024), BF),
            pltpu.VMEM((1, 1024), F32),
            pltpu.VMEM((8, TOP, 128, 128), F32),
            pltpu.VMEM((8, 128), F32),
            pltpu.VMEM((4, 8, 128), F32),
            pltpu.VMEM((8, 8, 128), F32),
            pltpu.VMEM((8, 128), F32),
            pltpu.VMEM((8, 8, 128), F32),
            dma, dma, dma, dma, dma((8, 3)), dma((8, 3)), dma((8, 3, 8)), dma((8, 3, 8)), dma((8, 3)),
            dma((8, 2)), dma((8, 2)), dma((8, 3, 4)), dma((8, 3, 4)),
            dma((4,)), dma((4,)), dma((8,)), dma((8,)), dma((8,)), dma((8,)),
            dma, dma((8,)),
        ],
        compiler_params=pltpu.CompilerParams(
            collective_id=0, has_side_effects=True, vmem_limit_bytes=50 * 1024 * 1024),
        cost_estimate=pl.CostEstimate(
            flops=3 * 2 * 1024 * 720 * 2880, bytes_accessed=20_000_000, transcendentals=0),
    )(ids, probs, og, weight, hidden)


def local(hidden_act, down_weight, out_grad, route_probs, expert_ids):
    wg, hg, pg = call(
        expert_ids.T, route_probs.T, out_grad.T, down_weight[0], hidden_act[0].T)
    return wg[None], hg.T[None], pg.T


def solution(mesh):
    return jax.shard_map(
        local,
        mesh=mesh,
        in_specs=(
            P("expert", None, "etp"),
            P("expert", "etp", None),
            P("expert", "etp"),
            P("expert", None),
            P("expert", None),
        ),
        out_specs=(P("expert", "etp", None), P("expert", None, "etp"), P("expert", None)),
        check_vma=False,
    )
```

```python
import jax
import jax.numpy as jnp
from jax import lax
from jax.experimental import pallas as pl
from jax.experimental.pallas import tpu as pltpu
from jax.sharding import PartitionSpec as P

BF = jnp.bfloat16
F32 = jnp.float32
MESH = pl.DeviceIdType.MESH

TOKENS = 128
TOP = 4
QUARTER = 720
WIDTH = 2880
CHUNK = 768
LATE = 512
EARLY = 256
META = 512
SLOT = 16
PLANES = 8
COLS = 4
PLANE = 8

SCHEDULE = (
    "T0", "K0", "K1", "K2", "K3", "K4", "K5", "K6", "K7", "N0", "S0", "A0", "E0", "Z1", "Z2", "A1",
    "A2", "C0", "Y1", "Y2", "E1", "E2", "F0", "N1", "Z3", "Z4", "A3", "A4", "C1", "C2", "N2", "Y3",
    "Y4", "E3", "E4", "F1", "F2", "Z5", "Z6", "A5", "A6", "C3", "C4", "N3", "Y5", "Y6", "E5", "E6",
    "D0", "F3", "F4", "Z7", "A7", "C5", "C6", "N4", "Y7", "E7", "D1", "F5", "F6", "N5", "C7", "F7",
    "D2", "B0", "W0", "D3", "D4", "B1", "W1", "D5", "M0", "M1", "D6", "B2", "D7", "B3", "R1", "W2",
    "M2", "R2", "W3", "M3", "M4", "M5", "R3", "H0", "H1", "H2", "H3", "R4",
)


def dot(a, b, ca, cb):
    return lax.dot_general(a, b, (((ca,), (cb,)), ((), ())), preferred_element_type=F32)


def iota(shape, dim):
    return lax.broadcasted_iota(jnp.int32, shape, dim)


def onehot(cond):
    return jnp.where(cond, 1.0, 0.0).astype(BF)


def keep(a0, a1, a2, a3):
    one, zero = jnp.ones((), BF), jnp.zeros((), BF)

    def wins(a, b):
        return jnp.where(a >= b, one, zero)

    def two(a, b, c):
        return jnp.maximum(jnp.minimum(a, b), jnp.minimum(c, jnp.maximum(a, b)))

    w01, w02, w03 = wins(a0, a1), wins(a0, a2), wins(a0, a3)
    w12, w13, w23 = wins(a1, a2), wins(a1, a3), wins(a2, a3)
    return (
        two(w01, w02, w03), two(one - w01, w12, w13),
        two(one - w02, one - w12, w23), two(one - w03, one - w13, one - w23))


def kernel(
    ids_ref, probs_ref, og_ref, w_hbm, hid_hbm,
    wg_ref, hg_ref, pg_ref,
    nb, zb0, zb1, sb0, sb1, dsel, fwd, bwd, up, down, rows, wv, wc, wr, rm, acc, hid, hsb, prs, kmask, sc, etp_in, pln_in, zout, zin,
    nb_s, nb_r, x_s, x_r, z_s, z_r, p_s, p_r, y_s, y_r, s_s, s_r,
    r1_s, r1_r, r2_s, r2_r, r3_s, r3_r, w_sem, hid_sem,
):
    e = lax.axis_index("expert")
    q = lax.axis_index("etp")
    z = e // PLANE
    x = (e // 2) % COLS
    yh = e % 2
    ylo, core = q // 2, q % 2
    q1 = ylo * 2 + 1 - core
    q2 = (1 - ylo) * 2 + core
    pending = []

    def send(src, dst, ss, rs, dev):
        cp = pltpu.make_async_remote_copy(src, dst, ss, rs, device_id=dev, device_id_type=MESH)
        cp.start()
        pending.append(cp)

    def arrived(ref, sem):
        pltpu.make_async_copy(ref, ref, sem).wait()

    def zdev(d):
        return (((z + d) % PLANES) * PLANE + e % PLANE, q)

    def rel(i):
        return -((i + 1) // 2) if i % 2 else i // 2

    rels = [(dx, dy) for dy in range(2) for dx in range(COLS) if (dx, dy) != (0, 0)]

    def plane_to(dx, dy):
        ex = z * PLANE + ((x + dx) % COLS) * 2 + (yh if dy == 0 else 1 - yh)
        return (ex, q if dy == 0 else q2)

    w_cp = pltpu.make_async_copy(w_hbm, wv, w_sem)
    w_cp.start()
    hid_cp = []
    for i in range(PLANES):
        src = (z + rel(i) + PLANES) % PLANES
        cp = pltpu.make_async_copy(
            hid_hbm.at[:, pl.ds(pl.multiple_of(src * 128, 128), 128)],
            hid.at[:, pl.ds(i * 128, 128)], hid_sem.at[i])
        cp.start()
        hid_cp.append(cp)

    peers = [zdev(d) for d in range(1, PLANES)]
    peers += [plane_to(dx, dy) for dx, dy in rels]
    peers += [(e, (q + d) % 4) for d in range(1, 4)]
    barrier = pltpu.get_barrier_semaphore()
    for dev in peers:
        pl.semaphore_signal(barrier, inc=1, device_id=dev, device_id_type=MESH)
    lane = iota((128, 128), 1)
    sub = iota((128, 128), 0)
    eye = lane == sub
    before = onehot(sub < lane)
    sub_expert = (sub // SLOT).astype(F32)
    sub_rank = (sub % SLOT).astype(F32)

    def column(r):
        return jnp.sum(jnp.where(eye, r, 0.0), axis=1, keepdims=True)

    def as_row(c):
        return jnp.sum(jnp.where(eye, c, 0.0), axis=0, keepdims=True)

    def routes(ids, plane):
        ex = sub_expert + (plane * PLANE).astype(F32)
        eqs = [ids[k:k + 1, :] == ex for k in range(TOP)]
        any_k = eqs[0] | eqs[1] | eqs[2] | eqs[3]
        rank = dot(onehot(any_k), before, 1, 0)
        return eqs, any_k, rank == sub_rank

    ids_f = ids_ref[...].astype(F32)
    diff = iota((QUARTER, LATE), 0) - iota((QUARTER, LATE), 1)
    zb0[0, 0:128, :] = dot(og_ref[...], onehot(diff == 48 * q), 0, 0).astype(BF)
    zb0[0, 128:144, 0:128] = jnp.concatenate([ids_f, jnp.zeros((12, 128), F32)], axis=0).astype(BF)
    zb0[0, 128:144, 128:LATE] = jnp.zeros((16, LATE - 128), BF)

    zbs = (zb0, zb1)

    def zsend(src, i, h, d):
        buf = zbs[h]
        send(buf.at[src], buf.at[i], z_s.at[i, h], z_r.at[i, h], zdev(d % PLANES))

    def step_s(_):
        pl.semaphore_wait(barrier, len(peers))
        send(og_ref.at[pl.ds(0, 144), :], nb, nb_s, nb_r, (e, (q + 3) % 4))
        zsend(0, 1, 0, 1)
        zsend(0, 2, 0, -1)

    probs = probs_ref[...]
    own_ids = [column(ids_f[k:k + 1, :]) for k in range(TOP)]
    own_probs = [column(probs[k:k + 1, :]) for k in range(TOP)]

    def meta(off):
        out = jnp.zeros((128, 128), F32)
        for k in range(TOP):
            hi = own_probs[k].astype(BF).astype(F32)
            rest = own_probs[k] - hi
            mid = rest.astype(BF).astype(F32)
            lo = rest - mid
            for part, v in enumerate((own_ids[k], hi, mid, lo)):
                out = out + jnp.where(lane == off + 4 * part + k, v, 0.0)
        return out

    def step_second():
        diff = iota((QUARTER, EARLY), 0) - iota((QUARTER, EARLY), 1)
        chunk = dot(og_ref[...], onehot(diff == 48 * q + LATE), 0, 0)
        last = jnp.where(q == 3, 1.0, 0.0)
        tile = last * meta(64)
        arrived(nb, nb_r)
        gap = jnp.where(q < 3, 48 * q - QUARTER + LATE, 100000)
        chunk = chunk + dot(nb[...], onehot(diff[:144] == gap), 0, 0)
        zb1[0, ylo] = jnp.concatenate(
            [chunk[:, 0:128] + tile, chunk[:, 128:256]], axis=1).astype(BF)
        send(zb1.at[0, ylo], zb1.at[0, ylo], x_s, x_r, (e, q2))

    late, early = pl.ds(0, LATE), pl.ds(LATE, EARLY)

    def come(i, h):
        arrived(zbs[h].at[i], z_r.at[i, h])
        if i in (1, 3) or (i == 5 and h == 0):
            zsend(i, i + 2, h, 1)
        if i in (2, 4):
            zsend(i, i + 2, h, -1)
        if i == 6 and h == 1:
            zsend(i, 7, h, -1)

    def to_plane(i, h, src, dst, sems):
        for dx, dy in rels:
            xt = (x + dx) % COLS
            yt = yh if dy == 0 else 1 - yh
            send(src.at[i, xt, yt], dst, p_s.at[i, h, dy * COLS + dx], sems[dy], plane_to(dx, dy))
        pltpu.make_async_copy(src.at[i, x, yh], dst, sems[0]).start()

    def step_a(i):
        _, any_k, hit = routes(zb0[i, 128:144, 0:128].astype(F32), z)
        dsel[i] = onehot(any_k & hit)
        picked = dot(dsel[i], zb0[i, 0:128, :], 1, 0)
        sb0[i] = picked.astype(BF).reshape(COLS, 2, SLOT, LATE)
        to_plane(i, 0, sb0, rows.at[i, x, yh, ylo, core, :, late], (p_r.at[i, 0], p_r.at[i, 1]))
        if i == 0:
            step_second()

    def step_e(i):
        if i == 0:
            arrived(zb1.at[0, 1 - ylo], x_r)
            zsend(0, 1, 1, 1)
            zsend(0, 2, 1, -1)
        for y in range(2):
            picked = dot(dsel[i], zb1[i, y], 1, 0)
            sb1[i, :, :, y] = picked.astype(BF).reshape(COLS, 2, SLOT, EARLY)
        to_plane(i, 1, sb1, rows.at[i, x, yh, :, core, :, early], (p_r.at[i, 2], p_r.at[i, 2]))

    def part(i, y, yl, c):
        return rows.at[i, :, y, yl, c, :, late]

    def both(i, c):
        return rows.at[i, :, :, :, c, :, early]

    def step_c(i):
        one, two = part(i, yh, ylo, core), part(i, 1 - yh, 1 - ylo, core)
        arrived(one, p_r.at[i, 0])
        send(one, one, y_s.at[i, 0], y_r.at[i, 0], (e, q2))
        arrived(two, p_r.at[i, 1])
        send(two, two, y_s.at[i, 1], y_r.at[i, 1], (e, q2))
        send(one, one, s_s.at[i, 0], s_r.at[i, 0], (e, q1))
        send(two, two, s_s.at[i, 1], s_r.at[i, 1], (e, q1))

    def step_f(i):
        arrived(both(i, core), p_r.at[i, 2])
        send(both(i, core), both(i, core), s_s.at[i, 4], s_r.at[i, 4], (e, q1))

    def step_d(i):
        one, two = part(i, yh, 1 - ylo, core), part(i, 1 - yh, ylo, core)
        arrived(one, y_r.at[i, 0])
        send(one, one, s_s.at[i, 2], s_r.at[i, 2], (e, q1))
        arrived(two, y_r.at[i, 1])
        send(two, two, s_s.at[i, 3], s_r.at[i, 3], (e, q1))

    def tables(_):
        f, c = iota((512, 512), 0), iota((512, 512), 1)
        fwd[...] = onehot((c % 128 == f // 4) & (c // 128 == f % 4))
        c, f = iota((512, 512), 0), iota((512, 512), 1)
        bwd[...] = onehot((c % 128 == f // 4) & (c // 128 == f % 4))
        c, f = iota((256, 240), 0), iota((256, 240), 1)
        up[...] = onehot((c % 64 == f // 4) & (c // 64 == f % 4))
        f, c = iota((240, 256), 0), iota((240, 256), 1)
        down[...] = onehot((c % 64 == f // 4) & (c // 64 == f % 4))
        w_cp.wait()

    def step_m(b):
        lo = 512 * b
        n = min(512, WIDTH - lo)
        wb = wv[:, lo:lo + n]
        a = jnp.abs(dot(wb, fwd[0:n, :], 1, 0)).astype(BF)
        kept = jnp.concatenate(keep(*[a[:, 128 * p:128 * p + 128] for p in range(4)]), axis=1)
        wc[:, lo:lo + n] = wb * dot(kept, bwd[:, 0:n], 1, 0).astype(BF)

    def step_n(b):
        lo = 512 * b
        n = min(512, WIDTH - lo)
        for m in range(3):
            at = slice(240 * m, 240 * m + 240)
            wb = wv[at, lo:lo + n]
            a = jnp.abs(dot(up[...], wb, 1, 0)).astype(BF)
            kept = jnp.concatenate(keep(*[a[64 * p:64 * p + 64] for p in range(4)]), axis=0)
            mask = dot(down[...], kept, 1, 0).astype(BF)
            rm[at, lo:lo + n] = mask
            wr[at, lo:lo + n] = wb * mask

    def step_k(i):
        eqs, _, hit = routes(ids_f, (z - rel(i) + PLANES) % PLANES)
        for k in range(TOP):
            kmask[i, k] = jnp.where(eqs[k] & hit, 1.0, 0.0)

    def r(g, qq, lo, n):
        return rows[2 * g:2 * g + 2, :, :, qq // 2, qq % 2, :, lo:lo + n].reshape(256, n)

    def wide_r(g):
        return jnp.concatenate(
            [r(g, c, 0, min(CHUNK, WIDTH - CHUNK * c)) for c in range(4)], axis=1)

    def span(g):
        return slice(256 * g, 256 * g + 256)

    def step_b(g):
        for i in (2 * g, 2 * g + 1):
            arrived(part(i, yh, ylo, 1 - core), s_r.at[i, 0])
            arrived(part(i, 1 - yh, 1 - ylo, 1 - core), s_r.at[i, 1])
            arrived(part(i, yh, 1 - ylo, 1 - core), s_r.at[i, 2])
            arrived(part(i, 1 - yh, ylo, 1 - core), s_r.at[i, 3])
            arrived(both(i, 1 - core), s_r.at[i, 4])
            hid_cp[i].wait()
        back = dot(wr[...], wide_r(g), 1, 1)
        score = jnp.sum(hid[:, span(g)].astype(F32) * back, axis=0, keepdims=True)
        sc[2 * g:2 * g + 1, :] = score[:, :128]
        sc[2 * g + 1:2 * g + 2, :] = score[:, 128:]

    def step_w(g):
        mt = r(g, 3, META, 128).astype(F32)
        total = pltpu.roll(mt, 124, 1) + pltpu.roll(mt, 120, 1) + pltpu.roll(mt, 116, 1)
        wide = iota((256, 128), 1)
        mine = (wide >= 64) & (wide < 68) & (mt == e.astype(F32))
        pc = jnp.sum(jnp.where(mine, total, 0.0), axis=1, keepdims=True)
        pr = jnp.concatenate([as_row(pc[:128]), as_row(pc[128:])], axis=1)
        prs[:, span(g)] = pr
        hsb[:, span(g)] = (hid[:, span(g)].astype(F32) * pr).astype(BF)
        for c in range(4):
            n = min(CHUNK, WIDTH - CHUNK * c)
            ln = slice(CHUNK * c, CHUNK * c + n)
            share = dot(hsb[:, span(g)], r(g, c, 0, n), 1, 0)
            if g > 0:
                share = share + acc[:, ln]
            if g < 3:
                acc[:, ln] = share
            else:
                wg_ref[:, ln] = jnp.where(rm[:, ln].astype(F32) > 0.5, share, 0.0).astype(BF)

    def step_h(g):
        grad = (dot(wc[...], wide_r(g), 1, 1) * prs[:, span(g)]).astype(BF)
        for i in (2 * g, 2 * g + 1):
            src = (z + rel(i) + PLANES) % PLANES
            at = 128 * (i % 2)
            hg_ref[:, pl.ds(pl.multiple_of(src * 128, 128), 128)] = grad[:, at:at + 128]

    def return_one():
        etp_in[q] = sc[...]
        for d in range(1, 4):
            send(etp_in.at[q], etp_in.at[q], r1_s.at[d], r1_r.at[d], (e, (q + d) % 4))

    def return_two():
        for d in range(1, 4):
            arrived(etp_in.at[(q - d + 4) % 4], r1_r.at[d])
        sc[...] = (etp_in[0] + etp_in[1]) + (etp_in[2] + etp_in[3])
        for dx, dy in rels:
            send(sc, pln_in.at[dy * COLS + dx], r2_s.at[dy * COLS + dx],
                 r2_r.at[dy * COLS + dx], plane_to(dx, dy))

    def return_three():
        lane8 = iota((8, 128), 1) // SLOT
        own = 2 * x + yh
        v = jnp.where(lane8 == own, sc[...], 0.0)
        for dx, dy in rels:
            arrived(pln_in.at[dy * COLS + dx], r2_r.at[dy * COLS + dx])
            sb = 2 * ((x - dx + COLS) % COLS) + (yh if dy == 0 else 1 - yh)
            shifted = pltpu.roll(pln_in[dy * COLS + dx], ((sb - own + PLANE) % PLANE) * SLOT, 1)
            v = v + jnp.where(lane8 == sb, shifted, 0.0)
        zout[...] = v
        for i in range(1, PLANES):
            send(zout, zin.at[i], r3_s.at[i], r3_r.at[i], zdev((rel(i) + PLANES) % PLANES))

    def return_four():
        totals = [jnp.zeros((128, 128), F32) for _ in range(TOP)]
        for i in range(PLANES):
            if i == 0:
                v = column(zout[0:1, :])
            else:
                arrived(zin.at[i], r3_r.at[i])
                v = column(zin[i, i:i + 1, :])
            for k in range(TOP):
                totals[k] = totals[k] + kmask[i, k] * v
        for k in range(TOP):
            pg_ref[k:k + 1, :] = jnp.sum(totals[k], axis=0, keepdims=True)

    steps = {"A": step_a, "C": step_c, "D": step_d, "E": step_e, "F": step_f, "M": step_m,
             "N": step_n, "Z": lambda i: come(i, 0), "Y": lambda i: come(i, 1), "T": tables, "S": step_s, "K": step_k, "B": step_b, "W": step_w, "H": step_h,
             "R": lambda n: (return_one, return_two, return_three, return_four)[n - 1]()}
    for item in SCHEDULE:
        steps[item[0]](int(item[1:]))
    for cp in pending:
        cp.wait_send()


def call(ids, probs, og, weight, hidden):
    hbm = pl.BlockSpec(memory_space=pltpu.HBM)
    out = pl.BlockSpec(memory_space=pltpu.VMEM)
    vmem = pl.BlockSpec(memory_space=pltpu.VMEM)
    dma = pltpu.SemaphoreType.DMA
    return pl.pallas_call(
        kernel,
        out_shape=(
            pltpu.VMEM((QUARTER, WIDTH), BF),
            pltpu.VMEM((QUARTER, 1024), BF),
            jax.ShapeDtypeStruct((TOP, TOKENS), F32),
        ),
        in_specs=[vmem, vmem, vmem, hbm, hbm],
        out_specs=(out, out, vmem),
        scratch_shapes=[
            pltpu.VMEM((144, TOKENS), BF),
            pltpu.VMEM((8, TOKENS + 16, LATE), BF),
            pltpu.VMEM((8, 2, TOKENS, EARLY), BF),
            pltpu.VMEM((8, COLS, 2, SLOT, LATE), BF),
            pltpu.VMEM((8, COLS, 2, 2, SLOT, EARLY), BF),
            pltpu.VMEM((8, 128, 128), BF),
            pltpu.VMEM((512, 512), BF),
            pltpu.VMEM((512, 512), BF),
            pltpu.VMEM((256, 240), BF),
            pltpu.VMEM((240, 256), BF),
            pltpu.VMEM((8, COLS, 2, 2, 2, SLOT, CHUNK), BF),
            pltpu.VMEM((QUARTER, WIDTH), BF),
            pltpu.VMEM((QUARTER, WIDTH), BF),
            pltpu.VMEM((QUARTER, WIDTH), BF),
            pltpu.VMEM((QUARTER, WIDTH), BF),
            pltpu.VMEM((QUARTER, WIDTH), F32),
            pltpu.VMEM((QUARTER, 1024), BF),
                pltpu.VMEM((QUARTER, 1024), BF),
            pltpu.VMEM((1, 1024), F32),
            pltpu.VMEM((8, TOP, 128, 128), F32),
            pltpu.VMEM((8, 128), F32),
            pltpu.VMEM((4, 8, 128), F32),
            pltpu.VMEM((8, 8, 128), F32),
            pltpu.VMEM((8, 128), F32),
            pltpu.VMEM((8, 8, 128), F32),
            dma, dma, dma, dma, dma((8, 2)), dma((8, 2)), dma((8, 2, 8)), dma((8, 3)),
            dma((8, 2)), dma((8, 2)), dma((8, 5)), dma((8, 5)),
            dma((4,)), dma((4,)), dma((8,)), dma((8,)), dma((8,)), dma((8,)),
            dma, dma((8,)),
        ],
        compiler_params=pltpu.CompilerParams(
            collective_id=0, has_side_effects=True, vmem_limit_bytes=50 * 1024 * 1024),
        cost_estimate=pl.CostEstimate(
            flops=3 * 2 * 1024 * 720 * 2880, bytes_accessed=20_000_000, transcendentals=0),
    )(ids, probs, og, weight, hidden)


def local(hidden_act, down_weight, out_grad, route_probs, expert_ids):
    wg, hg, pg = call(
        expert_ids.T, route_probs.T, out_grad.T, down_weight[0], hidden_act[0].T)
    return wg[None], hg.T[None], pg.T


def solution(mesh):
    return jax.shard_map(
        local,
        mesh=mesh,
        in_specs=(
            P("expert", None, "etp"),
            P("expert", "etp", None),
            P("expert", "etp"),
            P("expert", None),
            P("expert", None),
        ),
        out_specs=(P("expert", "etp", None), P("expert", None, "etp"), P("expert", None)),
        check_vma=False,
    )
```

```python
import jax
import jax.numpy as jnp
from jax import lax
from jax.experimental import pallas as pl
from jax.experimental.pallas import tpu as pltpu
from jax.sharding import PartitionSpec as P

BF = jnp.bfloat16
F32 = jnp.float32
MESH = pl.DeviceIdType.MESH

TOKENS = 128
TOP = 4
QUARTER = 720
WIDTH = 2880
CHUNK = 768
LATE = 512
EARLY = 256
META = 512
SLOT = 16
PLANES = 8
COLS = 4
PLANE = 8

SCHEDULE = (
    "T0", "K0", "K1", "K2", "K3", "K4", "K5", "K6", "K7", "N0", "N1", "S0", "A0", "N2", "N3", "E0",
    "Z1", "Z2", "A1", "A2", "Y1", "Y2", "C0", "E1", "E2", "Z3", "Z4", "F0", "A3", "A4", "C1", "C2",
    "Y3", "Y4", "E3", "E4", "F1", "F2", "Z5", "Z6", "A5", "A6", "C3", "C4", "Y5", "Y6", "E5", "E6",
    "F3", "F4", "Z7", "A7", "Y7", "E7", "D0", "C5", "C6", "F5", "F6", "N4", "D1", "N5", "C7", "F7",
    "D2", "B0", "W0", "D3", "D4", "B1", "W1", "D5", "M0", "M1", "D6", "B2", "D7", "B3", "R1", "W2",
    "M2", "R2", "W3", "M3", "M4", "M5", "R3", "H0", "H1", "H2", "H3", "R4",
)


def dot(a, b, ca, cb):
    return lax.dot_general(a, b, (((ca,), (cb,)), ((), ())), preferred_element_type=F32)


def iota(shape, dim):
    return lax.broadcasted_iota(jnp.int32, shape, dim)


def onehot(cond):
    return jnp.where(cond, 1.0, 0.0).astype(BF)


def keep(a0, a1, a2, a3):
    one, zero = jnp.ones((), BF), jnp.zeros((), BF)

    def wins(a, b):
        return jnp.where(a >= b, one, zero)

    def two(a, b, c):
        return jnp.maximum(jnp.minimum(a, b), jnp.minimum(c, jnp.maximum(a, b)))

    w01, w02, w03 = wins(a0, a1), wins(a0, a2), wins(a0, a3)
    w12, w13, w23 = wins(a1, a2), wins(a1, a3), wins(a2, a3)
    return (
        two(w01, w02, w03), two(one - w01, w12, w13),
        two(one - w02, one - w12, w23), two(one - w03, one - w13, one - w23))


def kernel(
    ids_ref, probs_ref, og_ref, w_hbm, hid_hbm,
    wg_ref, hg_ref, pg_ref,
    nb, zb0, zb1, sb0, sb1, dsel, fwd, bwd, up, down, rows, wv, wc, wr, rm, acc, hid, hsb, prs, kmask, sc, etp_in, pln_in, zout, zin,
    nb_s, nb_r, x_s, x_r, z_s, z_r, p_s, p_r, y_s, y_r, s_s, s_r,
    r1_s, r1_r, r2_s, r2_r, r3_s, r3_r, w_sem, hid_sem,
):
    e = lax.axis_index("expert")
    q = lax.axis_index("etp")
    z = e // PLANE
    x = (e // 2) % COLS
    yh = e % 2
    ylo, core = q // 2, q % 2
    q1 = ylo * 2 + 1 - core
    q2 = (1 - ylo) * 2 + core
    pending = []

    def send(src, dst, ss, rs, dev):
        cp = pltpu.make_async_remote_copy(src, dst, ss, rs, device_id=dev, device_id_type=MESH)
        cp.start()
        pending.append(cp)

    def arrived(ref, sem):
        pltpu.make_async_copy(ref, ref, sem).wait()

    def zdev(d):
        return (((z + d) % PLANES) * PLANE + e % PLANE, q)

    def rel(i):
        return -((i + 1) // 2) if i % 2 else i // 2

    rels = [(dx, dy) for dy in range(2) for dx in range(COLS) if (dx, dy) != (0, 0)]

    def plane_to(dx, dy):
        ex = z * PLANE + ((x + dx) % COLS) * 2 + (yh if dy == 0 else 1 - yh)
        return (ex, q if dy == 0 else q2)

    w_cp = pltpu.make_async_copy(w_hbm, wv, w_sem)
    w_cp.start()
    hid_cp = []
    for i in range(PLANES):
        src = (z + rel(i) + PLANES) % PLANES
        cp = pltpu.make_async_copy(
            hid_hbm.at[:, pl.ds(pl.multiple_of(src * 128, 128), 128)],
            hid.at[:, pl.ds(i * 128, 128)], hid_sem.at[i])
        cp.start()
        hid_cp.append(cp)

    peers = [zdev(d) for d in range(1, PLANES)]
    peers += [plane_to(dx, dy) for dx, dy in rels]
    peers += [(e, (q + d) % 4) for d in range(1, 4)]
    barrier = pltpu.get_barrier_semaphore()
    for dev in peers:
        pl.semaphore_signal(barrier, inc=1, device_id=dev, device_id_type=MESH)
    lane = iota((128, 128), 1)
    sub = iota((128, 128), 0)
    eye = lane == sub
    before = onehot(sub < lane)
    sub_expert = (sub // SLOT).astype(F32)
    sub_rank = (sub % SLOT).astype(F32)

    def column(r):
        return jnp.sum(jnp.where(eye, r, 0.0), axis=1, keepdims=True)

    def as_row(c):
        return jnp.sum(jnp.where(eye, c, 0.0), axis=0, keepdims=True)

    def routes(ids, plane):
        ex = sub_expert + (plane * PLANE).astype(F32)
        eqs = [ids[k:k + 1, :] == ex for k in range(TOP)]
        any_k = eqs[0] | eqs[1] | eqs[2] | eqs[3]
        rank = dot(onehot(any_k), before, 1, 0)
        return eqs, any_k, rank == sub_rank

    ids_f = ids_ref[...].astype(F32)
    diff = iota((QUARTER, LATE), 0) - iota((QUARTER, LATE), 1)
    zb0[0, 0:128, :] = dot(og_ref[...], onehot(diff == 48 * q), 0, 0).astype(BF)
    zb0[0, 128:144, 0:128] = jnp.concatenate([ids_f, jnp.zeros((12, 128), F32)], axis=0).astype(BF)
    zb0[0, 128:144, 128:LATE] = jnp.zeros((16, LATE - 128), BF)

    zbs = (zb0, zb1)

    def zsend(src, i, h, d):
        buf = zbs[h]
        send(buf.at[src], buf.at[i], z_s.at[i, h], z_r.at[i, h], zdev(d % PLANES))

    def step_s(_):
        pl.semaphore_wait(barrier, len(peers))
        send(og_ref.at[pl.ds(0, 144), :], nb, nb_s, nb_r, (e, (q + 3) % 4))
        zsend(0, 1, 0, 1)
        zsend(0, 2, 0, -1)

    probs = probs_ref[...]
    own_ids = [column(ids_f[k:k + 1, :]) for k in range(TOP)]
    own_probs = [column(probs[k:k + 1, :]) for k in range(TOP)]

    def meta(off):
        out = jnp.zeros((128, 128), F32)
        for k in range(TOP):
            hi = own_probs[k].astype(BF).astype(F32)
            rest = own_probs[k] - hi
            mid = rest.astype(BF).astype(F32)
            lo = rest - mid
            for part, v in enumerate((own_ids[k], hi, mid, lo)):
                out = out + jnp.where(lane == off + 4 * part + k, v, 0.0)
        return out

    def step_second():
        diff = iota((QUARTER, EARLY), 0) - iota((QUARTER, EARLY), 1)
        chunk = dot(og_ref[...], onehot(diff == 48 * q + LATE), 0, 0)
        last = jnp.where(q == 3, 1.0, 0.0)
        tile = last * meta(64)
        arrived(nb, nb_r)
        gap = jnp.where(q < 3, 48 * q - QUARTER + LATE, 100000)
        chunk = chunk + dot(nb[...], onehot(diff[:144] == gap), 0, 0)
        zb1[0, ylo] = jnp.concatenate(
            [chunk[:, 0:128] + tile, chunk[:, 128:256]], axis=1).astype(BF)
        send(zb1.at[0, ylo], zb1.at[0, ylo], x_s, x_r, (e, q2))

    late, early = pl.ds(0, LATE), pl.ds(LATE, EARLY)

    def come(i, h):
        arrived(zbs[h].at[i], z_r.at[i, h])
        if i in (1, 3) or (i == 5 and h == 0):
            zsend(i, i + 2, h, 1)
        if i in (2, 4):
            zsend(i, i + 2, h, -1)
        if i == 6 and h == 1:
            zsend(i, 7, h, -1)

    def to_plane(i, h, src, dst, sems):
        for dx, dy in rels:
            xt = (x + dx) % COLS
            yt = yh if dy == 0 else 1 - yh
            send(src.at[i, xt, yt], dst, p_s.at[i, h, dy * COLS + dx], sems[dy], plane_to(dx, dy))
        pltpu.make_async_copy(src.at[i, x, yh], dst, sems[0]).start()

    def step_a(i):
        _, any_k, hit = routes(zb0[i, 128:144, 0:128].astype(F32), z)
        dsel[i] = onehot(any_k & hit)
        picked = dot(dsel[i], zb0[i, 0:128, :], 1, 0)
        sb0[i] = picked.astype(BF).reshape(COLS, 2, SLOT, LATE)
        to_plane(i, 0, sb0, rows.at[i, x, yh, ylo, core, :, late], (p_r.at[i, 0], p_r.at[i, 1]))
        if i == 0:
            step_second()

    def step_e(i):
        if i == 0:
            arrived(zb1.at[0, 1 - ylo], x_r)
            zsend(0, 1, 1, 1)
            zsend(0, 2, 1, -1)
        for y in range(2):
            picked = dot(dsel[i], zb1[i, y], 1, 0)
            sb1[i, :, :, y] = picked.astype(BF).reshape(COLS, 2, SLOT, EARLY)
        to_plane(i, 1, sb1, rows.at[i, x, yh, :, core, :, early], (p_r.at[i, 2], p_r.at[i, 2]))

    def part(i, y, yl, c):
        return rows.at[i, :, y, yl, c, :, late]

    def both(i, c):
        return rows.at[i, :, :, :, c, :, early]

    def step_c(i):
        one, two = part(i, yh, ylo, core), part(i, 1 - yh, 1 - ylo, core)
        arrived(one, p_r.at[i, 0])
        send(one, one, y_s.at[i, 0], y_r.at[i, 0], (e, q2))
        arrived(two, p_r.at[i, 1])
        send(two, two, y_s.at[i, 1], y_r.at[i, 1], (e, q2))
        send(one, one, s_s.at[i, 0], s_r.at[i, 0], (e, q1))
        send(two, two, s_s.at[i, 1], s_r.at[i, 1], (e, q1))

    def step_f(i):
        arrived(both(i, core), p_r.at[i, 2])
        send(both(i, core), both(i, core), s_s.at[i, 4], s_r.at[i, 4], (e, q1))

    def step_d(i):
        one, two = part(i, yh, 1 - ylo, core), part(i, 1 - yh, ylo, core)
        arrived(one, y_r.at[i, 0])
        send(one, one, s_s.at[i, 2], s_r.at[i, 2], (e, q1))
        arrived(two, y_r.at[i, 1])
        send(two, two, s_s.at[i, 3], s_r.at[i, 3], (e, q1))

    def tables(_):
        f, c = iota((512, 512), 0), iota((512, 512), 1)
        fwd[...] = onehot((c % 128 == f // 4) & (c // 128 == f % 4))
        c, f = iota((512, 512), 0), iota((512, 512), 1)
        bwd[...] = onehot((c % 128 == f // 4) & (c // 128 == f % 4))
        c, f = iota((256, 240), 0), iota((256, 240), 1)
        up[...] = onehot((c % 64 == f // 4) & (c // 64 == f % 4))
        f, c = iota((240, 256), 0), iota((240, 256), 1)
        down[...] = onehot((c % 64 == f // 4) & (c // 64 == f % 4))
        w_cp.wait()

    def step_m(b):
        lo = 512 * b
        n = min(512, WIDTH - lo)
        wb = wv[:, lo:lo + n]
        a = jnp.abs(dot(wb, fwd[0:n, :], 1, 0)).astype(BF)
        kept = jnp.concatenate(keep(*[a[:, 128 * p:128 * p + 128] for p in range(4)]), axis=1)
        wc[:, lo:lo + n] = wb * dot(kept, bwd[:, 0:n], 1, 0).astype(BF)

    def step_n(b):
        lo = 512 * b
        n = min(512, WIDTH - lo)
        for m in range(3):
            at = slice(240 * m, 240 * m + 240)
            wb = wv[at, lo:lo + n]
            a = jnp.abs(dot(up[...], wb, 1, 0)).astype(BF)
            kept = jnp.concatenate(keep(*[a[64 * p:64 * p + 64] for p in range(4)]), axis=0)
            mask = dot(down[...], kept, 1, 0).astype(BF)
            rm[at, lo:lo + n] = mask
            wr[at, lo:lo + n] = wb * mask

    def step_k(i):
        eqs, _, hit = routes(ids_f, (z - rel(i) + PLANES) % PLANES)
        for k in range(TOP):
            kmask[i, k] = jnp.where(eqs[k] & hit, 1.0, 0.0)

    def r(g, qq, lo, n):
        return rows[2 * g:2 * g + 2, :, :, qq // 2, qq % 2, :, lo:lo + n].reshape(256, n)

    def wide_r(g):
        return jnp.concatenate(
            [r(g, c, 0, min(CHUNK, WIDTH - CHUNK * c)) for c in range(4)], axis=1)

    def span(g):
        return slice(256 * g, 256 * g + 256)

    def step_b(g):
        for i in (2 * g, 2 * g + 1):
            arrived(part(i, yh, ylo, 1 - core), s_r.at[i, 0])
            arrived(part(i, 1 - yh, 1 - ylo, 1 - core), s_r.at[i, 1])
            arrived(part(i, yh, 1 - ylo, 1 - core), s_r.at[i, 2])
            arrived(part(i, 1 - yh, ylo, 1 - core), s_r.at[i, 3])
            arrived(both(i, 1 - core), s_r.at[i, 4])
            hid_cp[i].wait()
        back = dot(wr[...], wide_r(g), 1, 1)
        score = jnp.sum(hid[:, span(g)].astype(F32) * back, axis=0, keepdims=True)
        sc[2 * g:2 * g + 1, :] = score[:, :128]
        sc[2 * g + 1:2 * g + 2, :] = score[:, 128:]

    def step_w(g):
        mt = r(g, 3, META, 128).astype(F32)
        total = pltpu.roll(mt, 124, 1) + pltpu.roll(mt, 120, 1) + pltpu.roll(mt, 116, 1)
        wide = iota((256, 128), 1)
        mine = (wide >= 64) & (wide < 68) & (mt == e.astype(F32))
        pc = jnp.sum(jnp.where(mine, total, 0.0), axis=1, keepdims=True)
        pr = jnp.concatenate([as_row(pc[:128]), as_row(pc[128:])], axis=1)
        prs[:, span(g)] = pr
        hsb[:, span(g)] = (hid[:, span(g)].astype(F32) * pr).astype(BF)
        for c in range(4):
            n = min(CHUNK, WIDTH - CHUNK * c)
            ln = slice(CHUNK * c, CHUNK * c + n)
            share = dot(hsb[:, span(g)], r(g, c, 0, n), 1, 0)
            if g > 0:
                share = share + acc[:, ln]
            if g < 3:
                acc[:, ln] = share
            else:
                wg_ref[:, ln] = jnp.where(rm[:, ln].astype(F32) > 0.5, share, 0.0).astype(BF)

    def step_h(g):
        grad = (dot(wc[...], wide_r(g), 1, 1) * prs[:, span(g)]).astype(BF)
        for i in (2 * g, 2 * g + 1):
            src = (z + rel(i) + PLANES) % PLANES
            at = 128 * (i % 2)
            hg_ref[:, pl.ds(pl.multiple_of(src * 128, 128), 128)] = grad[:, at:at + 128]

    def return_one():
        etp_in[q] = sc[...]
        for d in range(1, 4):
            send(etp_in.at[q], etp_in.at[q], r1_s.at[d], r1_r.at[d], (e, (q + d) % 4))

    def return_two():
        for d in range(1, 4):
            arrived(etp_in.at[(q - d + 4) % 4], r1_r.at[d])
        sc[...] = (etp_in[0] + etp_in[1]) + (etp_in[2] + etp_in[3])
        for dx, dy in rels:
            send(sc, pln_in.at[dy * COLS + dx], r2_s.at[dy * COLS + dx],
                 r2_r.at[dy * COLS + dx], plane_to(dx, dy))

    def return_three():
        lane8 = iota((8, 128), 1) // SLOT
        own = 2 * x + yh
        v = jnp.where(lane8 == own, sc[...], 0.0)
        for dx, dy in rels:
            arrived(pln_in.at[dy * COLS + dx], r2_r.at[dy * COLS + dx])
            sb = 2 * ((x - dx + COLS) % COLS) + (yh if dy == 0 else 1 - yh)
            shifted = pltpu.roll(pln_in[dy * COLS + dx], ((sb - own + PLANE) % PLANE) * SLOT, 1)
            v = v + jnp.where(lane8 == sb, shifted, 0.0)
        zout[...] = v
        for i in range(1, PLANES):
            send(zout, zin.at[i], r3_s.at[i], r3_r.at[i], zdev((rel(i) + PLANES) % PLANES))

    def return_four():
        totals = [jnp.zeros((128, 128), F32) for _ in range(TOP)]
        for i in range(PLANES):
            if i == 0:
                v = column(zout[0:1, :])
            else:
                arrived(zin.at[i], r3_r.at[i])
                v = column(zin[i, i:i + 1, :])
            for k in range(TOP):
                totals[k] = totals[k] + kmask[i, k] * v
        for k in range(TOP):
            pg_ref[k:k + 1, :] = jnp.sum(totals[k], axis=0, keepdims=True)

    steps = {"A": step_a, "C": step_c, "D": step_d, "E": step_e, "F": step_f, "M": step_m,
             "N": step_n, "Z": lambda i: come(i, 0), "Y": lambda i: come(i, 1), "T": tables, "S": step_s, "K": step_k, "B": step_b, "W": step_w, "H": step_h,
             "R": lambda n: (return_one, return_two, return_three, return_four)[n - 1]()}
    for item in SCHEDULE:
        steps[item[0]](int(item[1:]))
    for cp in pending:
        cp.wait_send()


def call(ids, probs, og, weight, hidden):
    hbm = pl.BlockSpec(memory_space=pltpu.HBM)
    out = pl.BlockSpec(memory_space=pltpu.VMEM)
    vmem = pl.BlockSpec(memory_space=pltpu.VMEM)
    dma = pltpu.SemaphoreType.DMA
    return pl.pallas_call(
        kernel,
        out_shape=(
            pltpu.VMEM((QUARTER, WIDTH), BF),
            pltpu.VMEM((QUARTER, 1024), BF),
            jax.ShapeDtypeStruct((TOP, TOKENS), F32),
        ),
        in_specs=[vmem, vmem, vmem, hbm, hbm],
        out_specs=(out, out, vmem),
        scratch_shapes=[
            pltpu.VMEM((144, TOKENS), BF),
            pltpu.VMEM((8, TOKENS + 16, LATE), BF),
            pltpu.VMEM((8, 2, TOKENS, EARLY), BF),
            pltpu.VMEM((8, COLS, 2, SLOT, LATE), BF),
            pltpu.VMEM((8, COLS, 2, 2, SLOT, EARLY), BF),
            pltpu.VMEM((8, 128, 128), BF),
            pltpu.VMEM((512, 512), BF),
            pltpu.VMEM((512, 512), BF),
            pltpu.VMEM((256, 240), BF),
            pltpu.VMEM((240, 256), BF),
            pltpu.VMEM((8, COLS, 2, 2, 2, SLOT, CHUNK), BF),
            pltpu.VMEM((QUARTER, WIDTH), BF),
            pltpu.VMEM((QUARTER, WIDTH), BF),
            pltpu.VMEM((QUARTER, WIDTH), BF),
            pltpu.VMEM((QUARTER, WIDTH), BF),
            pltpu.VMEM((QUARTER, WIDTH), F32),
            pltpu.VMEM((QUARTER, 1024), BF),
                pltpu.VMEM((QUARTER, 1024), BF),
            pltpu.VMEM((1, 1024), F32),
            pltpu.VMEM((8, TOP, 128, 128), F32),
            pltpu.VMEM((8, 128), F32),
            pltpu.VMEM((4, 8, 128), F32),
            pltpu.VMEM((8, 8, 128), F32),
            pltpu.VMEM((8, 128), F32),
            pltpu.VMEM((8, 8, 128), F32),
            dma, dma, dma, dma, dma((8, 2)), dma((8, 2)), dma((8, 2, 8)), dma((8, 3)),
            dma((8, 2)), dma((8, 2)), dma((8, 5)), dma((8, 5)),
            dma((4,)), dma((4,)), dma((8,)), dma((8,)), dma((8,)), dma((8,)),
            dma, dma((8,)),
        ],
        compiler_params=pltpu.CompilerParams(
            collective_id=0, has_side_effects=True, vmem_limit_bytes=50 * 1024 * 1024),
        cost_estimate=pl.CostEstimate(
            flops=3 * 2 * 1024 * 720 * 2880, bytes_accessed=20_000_000, transcendentals=0),
    )(ids, probs, og, weight, hidden)


def local(hidden_act, down_weight, out_grad, route_probs, expert_ids):
    wg, hg, pg = call(
        expert_ids.T, route_probs.T, out_grad.T, down_weight[0], hidden_act[0].T)
    return wg[None], hg.T[None], pg.T


def solution(mesh):
    return jax.shard_map(
        local,
        mesh=mesh,
        in_specs=(
            P("expert", None, "etp"),
            P("expert", "etp", None),
            P("expert", "etp"),
            P("expert", None),
            P("expert", None),
        ),
        out_specs=(P("expert", "etp", None), P("expert", None, "etp"), P("expert", None)),
        check_vma=False,
    )
```
